512 devices in a mesh: dp: 4 (over y), blk: 16 (over z_lo, x), uly: 8 (over z_hi, core).
Axes of the slice: x: 4, y: 4, z: 16 (z_hi: 4, z_lo: 4; z = z_hi * 4 + z_lo), core: 2. Of those that a mesh axis runs over, the one named last changes fastest.
Arguments:
- queries: bfloat16 [4, 16384, 4096], P('dp', ('blk', 'uly')), may hold values from -6 to 6
- keys: bfloat16 [4, 16384, 512], P('dp', ('blk', 'uly')), may hold values from -6 to 6
- values: bfloat16 [4, 16384, 512], P('dp', ('blk', 'uly')), may hold values from -6 to 6
- output_gradient: bfloat16 [4, 16384, 4096], P('dp', ('blk', 'uly')), may hold values from -6 to 6
- layer_input: bfloat16 [4, 16384, 8192], P('dp', ('blk', 'uly')), may hold values from -6 to 6
- saved_log_total: float32 [4, 32, 16384], P('dp', 'uly', 'blk'), may hold values from 4 to 7
- row_dot_products: float32 [4, 32, 16384], P('dp', 'uly', 'blk'), may hold values from -6 to 6
- segment_ids: int32 [4, 16384], P('dp'), may hold values from 0 to 63, never falling along the last dimension, each value on 1 to 384 neighbouring positions
- tenants: int32 [4], P('dp'), may hold values from 0 to 3
- adapter_down: bfloat16 [4, 8192, 16], P(None, ('blk', 'uly')), may hold values from -0.0625 to 0.0625
- adapter_up: bfloat16 [4, 16, 4096], P(None, None, 'uly'), may hold values from -1.5 to 1.5
Outputs:
- key_grad: bfloat16 [4, 16384, 512], P('dp', ('blk', 'uly'))
- value_grad: bfloat16 [4, 16384, 512], P('dp', ('blk', 'uly'))
- down_grad: float32 [4, 8192, 16], P(None, ('blk', 'uly'))
- up_grad: float32 [4, 16, 4096], P(None, None, 'uly')
The draws below stay inside these ranges and needn't reach their ends.
Inputs may be any that keep to these rules, and one draw needn't show every extreme that they name: `segment_ids`: documents are runs of consecutive tokens numbered in order. `tenants`: several sequences may use one adapter.
All inputs are finite; a program needn't handle non-finite values.
Results may differ from the reference program's by a relative error of at most 0.012.
Values may be sent and summed in bfloat16 or wider, within the bound.
A program may use at most 64 MiB of HBM per device.

```python
import math
import jax
import jax.numpy as jnp
import numpy as np
from jax import lax

D = 8192
HEAD_SIZE = 128
QUERY_HEADS = 32
KEY_VALUE_HEADS = 4
R = 16
TEN = 4
TENANT_GROUPS = 4
SEQUENCE_TOKENS = 16384
WINDOW_TOKENS = 128
N_BLK = 16
N_ULY = 8


def set_ends(drawn, rng, low, high):
    place = [jax.random.randint(jax.random.fold_in(rng, axis), (), 0, length) for axis, length in enumerate(drawn.shape)]
    main_axis = drawn.shape.index(max(drawn.shape))
    beside = place[:main_axis] + [(place[main_axis] + 1) % drawn.shape[main_axis]] + place[main_axis + 1:]
    return drawn.at[tuple(place)].set(low).at[tuple(beside)].set(high)


def block_levels(rng, dims, pieces, low, top_value):
    loudness = 1.0
    for position, blocks in pieces:
        heights = jax.random.uniform(jax.random.fold_in(jax.random.fold_in(rng, 6), position), (blocks,), jnp.float32, low / len(pieces), top_value / len(pieces))
        loudness = loudness * jnp.repeat(jnp.exp(heights), dims[position] // blocks).reshape((-1,) + (1,) * (len(dims) - 1 - position))
    return loudness


def profile(amount, total, reach, skew):
    loads = [(1 << 20) // math.isqrt(standing ** skew) + 1 for standing in range(2, amount + 1)]
    rest, given = total - reach - (amount - 1), [1] * (amount - 1)
    while rest > 0:
        candidates = [i for i in range(amount - 1) if given[i] < reach]
        pool, remaining = sum([loads[i] for i in candidates]), rest
        for i in candidates:
            addition = min(reach - given[i], max(1, remaining * loads[i] // pool), rest)
            given[i] = given[i] + addition
            rest = rest - addition
    return np.array([reach] + given)


def uneven(stream_key, amount, total, bound, skew):
    if amount == 2:
        one = jax.random.randint(stream_key, (), max(1, total - bound), min(bound, total - 1) + 1)
        return jnp.stack([one, total - one])
    lengths = jnp.asarray(profile(amount, total, bound, skew), jnp.int32)
    pairs = (amount - 1) // 2
    source_of, sink = lengths[1:1 + 2 * pairs:2], lengths[2:2 + 2 * pairs:2]
    margin = jnp.minimum(source_of - 1, bound - sink)
    moved = jax.random.randint(jax.random.fold_in(stream_key, 1), (pairs,), 0, 1 << 20) % (margin + 1)
    lengths = lengths.at[1:1 + 2 * pairs:2].set(source_of - moved).at[2:2 + 2 * pairs:2].set(sink + moved)
    return lengths[jax.random.permutation(jax.random.fold_in(stream_key, 2), amount)]


def bell_draw(own_key, shape, spread, reach, pieces=(), held_as=jnp.bfloat16):
    array = jax.random.normal(own_key, shape, jnp.float32) * spread
    if len(pieces) > 0:
        array = block_levels(own_key, shape, pieces, -0.22, 0.18) * array
    return jnp.clip(array, min=-reach, max=reach).astype(held_as)


def setup_inputs(seed: int = 0) -> dict:
    key_list = jax.random.split(jax.random.key(seed), 12)
    return {
        "queries": bell_draw(key_list[0], (TENANT_GROUPS, SEQUENCE_TOKENS, QUERY_HEADS * HEAD_SIZE), 1.0, 6.0, ((0, 4), (1, 128))),
        "keys": bell_draw(key_list[1], (TENANT_GROUPS, SEQUENCE_TOKENS, KEY_VALUE_HEADS * HEAD_SIZE), 1.0, 6.0, ((0, 4), (1, 128))),
        "values": bell_draw(key_list[2], (TENANT_GROUPS, SEQUENCE_TOKENS, KEY_VALUE_HEADS * HEAD_SIZE), 1.0, 6.0, ((0, 4), (1, 128))),
        "output_gradient": bell_draw(key_list[3], (TENANT_GROUPS, SEQUENCE_TOKENS, QUERY_HEADS * HEAD_SIZE), 1.0, 6.0, ((0, 4), (1, 128))),
        "layer_input": bell_draw(key_list[4], (TENANT_GROUPS, SEQUENCE_TOKENS, D), 1.0, 6.0, ((0, 4), (1, 128))),
        "saved_log_total": jnp.clip(4.0 + 3.0 * jax.random.uniform(key_list[5], (TENANT_GROUPS, QUERY_HEADS, SEQUENCE_TOKENS), jnp.float32) ** block_levels(key_list[5], (TENANT_GROUPS, QUERY_HEADS, SEQUENCE_TOKENS), ((0, 4), (1, 8), (2, 16)), -0.2, 0.2), 4.0, 7.0),
        "row_dot_products": bell_draw(key_list[6], (TENANT_GROUPS, QUERY_HEADS, SEQUENCE_TOKENS), 1.0, 6.0, ((0, 4), (1, 8), (2, 16)), jnp.float32),
        "segment_ids": jax.vmap(lambda own: jnp.searchsorted(jnp.cumsum(uneven(own, N_BLK * N_ULY // 2, SEQUENCE_TOKENS, 3 * WINDOW_TOKENS, 1)), jnp.arange(SEQUENCE_TOKENS), side="right"))(jax.random.split(key_list[7], TENANT_GROUPS)).reshape((TENANT_GROUPS, SEQUENCE_TOKENS)).astype(jnp.int32),
        "tenants": set_ends(jax.random.randint(key_list[8], (TENANT_GROUPS,), 0, TEN), jax.random.fold_in(key_list[8], 1), 0, TEN - 1).astype(jnp.int32),
        "adapter_down": bell_draw(key_list[9], (TEN, D, R), D ** -0.5, 0.0625, ((1, 128),)),
        "adapter_up": bell_draw(key_list[10], (TEN, R, QUERY_HEADS * HEAD_SIZE), R ** -0.5, 1.5, ((2, 8),)),
    }


ADAPTER_SCALE = 2.0


def tile_grads(q_s, g_s, lse_s, dots_s, k_s, v_s, allowed, scale):
    hi = lax.Precision.HIGHEST
    qf = q_s.astype(jnp.float32)
    gf = g_s.astype(jnp.float32)
    kf = k_s.astype(jnp.float32)
    vf = v_s.astype(jnp.float32)
    scores = jnp.einsum('rkgd,ckd->kgrc', qf, kf, precision=hi) * scale
    probs = jnp.where(allowed, jnp.exp(scores - lse_s[..., None]), 0.0)
    probs_low = probs.astype(jnp.bfloat16).astype(jnp.float32)
    value_part = jnp.einsum('kgrc,rkgd->ckd', probs_low, gf, precision=hi)
    prob_grad = jnp.einsum('rkgd,ckd->kgrc', gf, vf, precision=hi)
    score_grad = (probs * (prob_grad - dots_s[..., None])).astype(jnp.bfloat16).astype(jnp.float32)
    query_part = jnp.einsum('kgrc,ckd->rkgd', score_grad, kf, precision=hi) * scale
    key_part = jnp.einsum('kgrc,rkgd->ckd', score_grad, qf, precision=hi) * scale
    return query_part, key_part, value_part


def reference(queries, keys, values, output_gradient, layer_input, saved_log_total, row_dot_products, segment_ids, tenants, adapter_down, adapter_up):
    scale = HEAD_SIZE ** -0.5
    group_width = QUERY_HEADS // KEY_VALUE_HEADS
    block_list = SEQUENCE_TOKENS // WINDOW_TOKENS
    rows = jnp.arange(WINDOW_TOKENS)
    lower = rows[None, :] <= rows[:, None]
    upper = rows[:, None] < rows[None, :]

    def one_group(block_index):
        query_slice = queries[block_index].reshape(block_list, WINDOW_TOKENS, KEY_VALUE_HEADS, group_width, HEAD_SIZE)
        gradient_slice = output_gradient[block_index].reshape(block_list, WINDOW_TOKENS, KEY_VALUE_HEADS, group_width, HEAD_SIZE)
        key_slice = keys[block_index].reshape(block_list, WINDOW_TOKENS, KEY_VALUE_HEADS, HEAD_SIZE)
        value_slice = values[block_index].reshape(block_list, WINDOW_TOKENS, KEY_VALUE_HEADS, HEAD_SIZE)
        log_total = saved_log_total[block_index].reshape(KEY_VALUE_HEADS, group_width, block_list, WINDOW_TOKENS)
        dot_products = row_dot_products[block_index].reshape(KEY_VALUE_HEADS, group_width, block_list, WINDOW_TOKENS)
        seg = segment_ids[block_index].reshape(block_list, WINDOW_TOKENS)

        def sub_block(step):
            before = jnp.maximum(step - 1, 0)
            seg_now = seg[step]
            seg_before = seg[before]
            own = tile_grads(query_slice[step], gradient_slice[step], log_total[:, :, step], dot_products[:, :, step], key_slice[step], value_slice[step],
                             lower & (seg_now[:, None] == seg_now[None, :]), scale)
            back = tile_grads(query_slice[step], gradient_slice[step], log_total[:, :, step], dot_products[:, :, step], key_slice[before], value_slice[before],
                              upper & (seg_now[:, None] == seg_before[None, :]) & (step > 0), scale)
            return own[0] + back[0], own[1], own[2], back[1], back[2]

        dq, dk_own, dv_own, dk_back, dv_back = lax.map(sub_block, jnp.arange(block_list))
        key_gradient = dk_own + jnp.concatenate([dk_back[1:], jnp.zeros_like(dk_back[:1])], axis=0)
        value_gradient = dv_own + jnp.concatenate([dv_back[1:], jnp.zeros_like(dv_back[:1])], axis=0)
        query_gradient = dq.reshape(SEQUENCE_TOKENS, QUERY_HEADS * HEAD_SIZE).astype(jnp.bfloat16)
        key_result = key_gradient.reshape(SEQUENCE_TOKENS, KEY_VALUE_HEADS * HEAD_SIZE).astype(jnp.bfloat16)
        value_result = value_gradient.reshape(SEQUENCE_TOKENS, KEY_VALUE_HEADS * HEAD_SIZE).astype(jnp.bfloat16)
        tenant = tenants[block_index]
        down_sel = adapter_down[tenant]
        upward_selected = adapter_up[tenant]
        xrow = layer_input[block_index]
        adapter_lower = jnp.dot(xrow, down_sel, preferred_element_type=jnp.float32).astype(jnp.bfloat16)
        coefficient = (ADAPTER_SCALE * jnp.dot(query_gradient, upward_selected.T, preferred_element_type=jnp.float32)).astype(jnp.bfloat16)
        down_part = jnp.dot(xrow.T, coefficient, preferred_element_type=jnp.float32)
        upward_partial = ADAPTER_SCALE * jnp.dot(adapter_lower.T, query_gradient, preferred_element_type=jnp.float32)
        hot = (jnp.arange(TEN) == tenant).astype(jnp.float32)
        return key_result, value_result, hot[:, None, None] * down_part[None], hot[:, None, None] * upward_partial[None]

    key_grad, value_grad, down_all, up_all = lax.map(one_group, jnp.arange(TENANT_GROUPS))
    return key_grad, value_grad, jnp.sum(down_all, axis=0), jnp.sum(up_all, axis=0)
```

```python
import jax
import jax.numpy as jnp
from jax import lax
from jax.experimental import pallas as pl
from jax.experimental.pallas import tpu as pltpu
from jax.sharding import PartitionSpec as P

MESH = pl.DeviceIdType.MESH
F32 = jnp.float32
BF16 = jnp.bfloat16

HEAD = 128
HEADS = 32
KV = 4
GROUP = HEADS // KV
TEN = 4
R = 16
TOK = 128
D = 8192
SEQ = 16384
WIDE = HEADS * HEAD
SCALE = HEAD ** -0.5
LOG2E = 1.4426950408889634
ADAPTER_SCALE = 2.0
NT = (((1,), (1,)), ((), ()))
NN = (((1,), (0,)), ((), ()))
TN = (((0,), (0,)), ((), ()))


def dot(a, b, dims):
    return lax.dot_general(a, b, dims, preferred_element_type=F32)


def mod(a, n):
    return lax.rem(a, jnp.int32(n))


def div(a, n):
    return lax.div(a, jnp.int32(n))


class Sems:
    def __init__(self):
        self.count = 0

    def take(self, n):
        first = self.count
        self.count += n
        return first


def layout():
    s = Sems()
    names = dict(
        ld=7, kv=4, dkv=4, au=7, ten=3, a2=15, u3=3, cu=1, cd=1, xu=3, xd=3,
        zhu=3, zhd=3, zlu=3, zld=3, xyu=15, xyd=3,
    )
    return {name: s.take(n) for name, n in names.items()}, s.count


SEM, N_SEM = layout()
L_KV, L_LD, L_SEG, L_ADN, L_AUP, L_Q, L_G, L_X, L_OUT, N_LOC = 0, 8, 10, 12, 13, 14, 15, 16, 17, 21


def kernel(
    ten_s, q_h, k_h, v_h, g_h, x_h, lse_h, dots_h, seg_h, adn_h, aup_h,
    kg_o, vg_o, down_o, up_o,
    q_v, g_v, x_v, kv_v, halo, ld_v, ld_all, seg_v, adn_v, aup_v, bias_v,
    dkv_own, dkv_out, dkv_in, dqt, au, ag, ug, ten_v,
    s1u, s1d, rcu, rcd, s2u, s2d, rxu, rxd, s3u, s3d, rhu, rhd, s4u, s4d, rlu, rld, fu, fd, kg_v, vg_v, down_v, up_v,
    loc, ssem, rsem,
):
    y = lax.axis_index("dp")
    b = lax.axis_index("blk")
    u = lax.axis_index("uly")
    zl, x = div(b, 4), mod(b, 4)
    zh, c = div(u, 2), mod(u, 2)
    t = b * 8 + u

    def dev(y_=y, zl_=zl, x_=x, zh_=zh, c_=c):
        return (y_, zl_ * 4 + x_, zh_ * 2 + c_)

    def token_dev(t_):
        return (y, div(t_, 8), mod(t_, 8))

    following = token_dev(mod(t + 1, 128))
    previous = token_dev(mod(t + 127, 128))

    def local(src, dst, i):
        return pltpu.make_async_copy(src, dst, loc.at[i])

    def remote(src, dst, i, to):
        return pltpu.make_async_remote_copy(
            src_ref=src, dst_ref=dst, send_sem=ssem.at[i], recv_sem=rsem.at[i], device_id=to, device_id_type=MESH
        )

    peers = [previous, following]
    peers += [dev(zh_=mod(zh + k, 4)) for k in (1, 2, 3)]
    peers += [dev(zh_=mod(zh + k, 4), c_=1 - c) for k in (0, 1, 2, 3)]
    plane = [(i, j) for i in range(4) for j in range(4) if (i, j) != (0, 0)]
    peers += [dev(zl_=mod(zl + i, 4), x_=mod(x + j, 4)) for i, j in plane]
    peers += [dev(y_=mod(y + i, 4), x_=mod(x + j, 4)) for i, j in plane if i != 0]
    barrier = pltpu.get_barrier_semaphore()
    for to in peers:
        pl.semaphore_signal(barrier, inc=1, device_id=to, device_id_type=MESH)

    small = [
        local(adn_h, adn_v, L_ADN),
        local(aup_h, aup_v, L_AUP),
        local(lse_h.at[0], ld_v.at[0], L_LD),
        local(dots_h.at[0], ld_v.at[1], L_LD + 1),
        local(seg_h.at[:, pl.ds(pl.multiple_of(t * TOK, TOK), TOK)], seg_v.at[1], L_SEG),
        local(seg_h.at[:, pl.ds(pl.multiple_of(mod(t + 127, 128) * TOK, TOK), TOK)], seg_v.at[0], L_SEG + 1),
    ]
    kv_loads = []
    for i in range(KV):
        kv_loads.append(local(k_h.at[0, :, pl.ds(i * HEAD, HEAD)], kv_v.at[i, 0], L_KV + 2 * i))
        kv_loads.append(local(v_h.at[0, :, pl.ds(i * HEAD, HEAD)], kv_v.at[i, 1], L_KV + 2 * i + 1))
    big = [local(q_h.at[0], q_v, L_Q), local(g_h.at[0], g_v, L_G)]
    x_load = local(x_h.at[0], x_v, L_X)
    for copy in small + kv_loads + big + [x_load]:
        copy.start()

    for copy in small:
        copy.wait()
    tenant = jnp.full((R, 128), ten_s[0], jnp.int32)
    ten_v[y] = tenant.astype(F32).astype(BF16)
    down_sel = jnp.zeros((R, 64), F32)
    up_sel = jnp.zeros((R, 128), F32)
    for a in range(TEN):
        down_sel += jnp.where(tenant[:, :64] == a, adn_v[a].astype(F32), 0.0)
        up_sel += jnp.where(tenant == a, aup_v[a, :, pl.ds(pl.multiple_of(x * 128, 128), 128)].astype(F32), 0.0)
    place = lax.broadcasted_iota(jnp.int32, (64, 128), 1) - lax.broadcasted_iota(jnp.int32, (64, 128), 0)
    shift = jnp.where(place == c * 64, 1.0, 0.0).astype(BF16)
    au[u, 0] = dot(down_sel.astype(BF16), shift, NN).astype(BF16)
    au[u, 1] = up_sel.astype(BF16)
    ld_all[u] = ld_v[:, :, pl.ds(pl.multiple_of(u * TOK, TOK), TOK)]
    row = lax.broadcasted_iota(jnp.int32, (TOK, TOK), 0)
    col = lax.broadcasted_iota(jnp.int32, (TOK, TOK), 1)
    ids_now = jnp.broadcast_to(seg_v[1].astype(F32), (TOK, TOK))
    ids_before = jnp.broadcast_to(seg_v[0].astype(F32), (TOK, TOK))
    now_rows = jnp.sum(jnp.where(row == col, ids_now, 0.0), axis=1, keepdims=True)
    before_rows = jnp.sum(jnp.where(row == col, ids_before, 0.0), axis=1, keepdims=True)
    first = jnp.broadcast_to(t, (TOK, TOK)) > 0
    bias_v[:TOK] = jnp.where((row > col) & (before_rows == ids_now) & first, 0.0, -1e30)
    bias_v[TOK:] = jnp.where((row <= col) & (now_rows == ids_now), 0.0, -1e30)

    for copy in kv_loads:
        copy.wait()
    pl.semaphore_wait(barrier, len(peers))

    sent = []

    def go(copy):
        copy.start()
        sent.append(copy)
        return copy

    other_core = dev(c_=1 - c)
    au_copies, ld_copies = [], []
    others = [(k, other) for k in (2, 1, 3, 0) for other in (0, 1) if (k, other) != (0, 0)]
    for n, (k, other) in enumerate(others):
        to = dev(zh_=mod(zh + k, 4), c_=(1 - c) if other else c)
        au_copies.append(go(remote(au.at[u], au.at[u], SEM["au"] + n, to)))
    for n, (k, other) in enumerate(others):
        zh_to = mod(zh + k, 4)
        c_to = (1 - c) if other else c
        piece = pl.ds(pl.multiple_of((zh_to * 2 + c_to) * TOK, TOK), TOK)
        ld_copies.append(go(remote(ld_v.at[:, :, piece], ld_all.at[u], SEM["ld"] + n, dev(zh_=zh_to, c_=c_to))))
    kv_copies = [go(remote(kv_v.at[i], halo.at[i], SEM["kv"] + i, following)) for i in range(KV)]
    tens = [
        go(remote(ten_v.at[y], ten_v.at[y], SEM["ten"] + k - 1, dev(y_=mod(y + k, 4)))) for k in (1, 2, 3)
    ]

    for copy in au_copies:
        copy.wait_recv()
    for j in range(4):
        ag[zl, x, j] = au[2 * j, 0] + au[2 * j + 1, 0]
    for j in range(8):
        ug[x, j] = au[j, 1]
    a2 = []
    for n, (i, j) in enumerate(plane):
        to = dev(zl_=mod(zl + i, 4), x_=mod(x + j, 4))
        a2.append(go(remote(ag.at[zl, x], ag.at[zl, x], SEM["a2"] + n, to)))
    u3 = [go(remote(ug.at[x], ug.at[x], SEM["u3"] + k - 1, dev(x_=mod(x + k, 4)))) for k in (1, 2, 3)]
    for copy in big:
        copy.wait()
    for copy in ld_copies:
        copy.wait_recv()

    def one_head(i):
        keys = jnp.concatenate([halo[i, 0], kv_v[i, 0]], axis=0)
        values = jnp.concatenate([halo[i, 1], kv_v[i, 1]], axis=0)
        q_list, g_list, p_list, s_list = [], [], [], []
        for half in range(2):
            heads = range(half * 4, half * 4 + 4)
            q = jnp.concatenate([q_v[:, (i * GROUP + h) * HEAD:(i * GROUP + h + 1) * HEAD] for h in heads], axis=0)
            g = jnp.concatenate([g_v[:, (i * GROUP + h) * HEAD:(i * GROUP + h + 1) * HEAD] for h in heads], axis=0)
            scores = dot(keys, q, NT)
            grads = dot(values, g, NT)
            q_list.append(q)
            g_list.append(g)
            for n in range(4):
                at = slice(n * TOK, (n + 1) * TOK)
                lse = ld_all[2 * i + half, 0, n:n + 1] * LOG2E
                dots = ld_all[2 * i + half, 1, n:n + 1]
                probs = jnp.exp2((scores[:, at] * (SCALE * LOG2E) - lse) + bias_v[...])
                p_list.append(probs.astype(BF16))
                s_list.append((probs * (grads[:, at] - dots)).astype(BF16))
        score_grad = jnp.concatenate(s_list, axis=1)
        value_part = dot(jnp.concatenate(p_list, axis=1), jnp.concatenate(g_list, axis=0), NN)
        key_part = dot(score_grad, jnp.concatenate(q_list, axis=0), NN) * SCALE
        query_part = (dot(keys, score_grad, TN) * SCALE).astype(BF16)
        dkv_out[i, 0] = key_part[:TOK].astype(BF16)
        dkv_out[i, 1] = value_part[:TOK].astype(BF16)
        dkv_own[i, 0] = key_part[TOK:]
        dkv_own[i, 1] = value_part[TOK:]
        for h in range(GROUP):
            dqt[(i * GROUP + h) * HEAD:(i * GROUP + h + 1) * HEAD] = query_part[:, h * HEAD:(h + 1) * HEAD]

    dkv_copies = [remote(dkv_out.at[i], dkv_in.at[i], SEM["dkv"] + i, previous) for i in range(KV)]

    for i in range(KV):
        kv_copies[i].wait_recv()
        one_head(i)
        go(dkv_copies[i])

    for copy in u3:
        copy.wait_recv()
    x_load.wait()

    def to_three(name, source, target, place, axis):
        copies = []
        for k in (2, 1, 3):
            to = mod(place + k, 4)
            copies.append(go(remote(source(to), target.at[k - 1], SEM[name] + k - 1, dev(**{axis: to}))))
        return copies

    def sum_of_four(own, target, copies):
        total = own.astype(F32)
        for k, copy in zip((2, 1, 3), copies):
            copy.wait_recv()
            total += target[k - 1].astype(F32)
        return total.astype(BF16)

    up_rows = jnp.concatenate([ug[k, n] for n in range(8) for k in range(4)], axis=1)
    coeff = (ADAPTER_SCALE * dot(up_rows, dqt[...], NN)).astype(BF16)
    left = lax.broadcasted_iota(jnp.int32, (R, 128), 1) < 64
    for m in range(2):
        part = dot(coeff, x_v[:, m * 4096:(m + 1) * 4096], NN)
        for n in range(4):
            for j in range(4):
                a = part[:, (n * 4 + j) * 128:(n * 4 + j + 1) * 128]
                d = part[:, 2048 + (n * 4 + j) * 128:2048 + (n * 4 + j + 1) * 128]
                s1d[0, n, j, m] = jnp.where(left, a, pltpu.roll(d, 64, 1)).astype(BF16)
                s1d[1, n, j, m] = jnp.where(left, pltpu.roll(a, 64, 1), d).astype(BF16)
    cd = go(remote(s1d.at[1 - c], rcd, SEM["cd"], other_core))

    cd.wait_recv()
    s2d[...] = (s1d[c].astype(F32) + rcd[...].astype(F32)).astype(BF16)
    xd = to_three("xd", lambda to: s2d.at[to], rxd, x, "x_")

    for copy in a2:
        copy.wait_recv()
    down_rows = jnp.concatenate([ag[i, j, k] for i in range(4) for j in range(4) for k in range(4)], axis=1)
    low = (ADAPTER_SCALE * dot(down_rows, x_v[...], NT).astype(BF16).astype(F32)).astype(BF16)
    for n in range(KV):
        part = dot(low, dqt[n * 1024:(n + 1) * 1024], NT)
        for j in range(2):
            for k in range(4):
                s1u[j, k, n] = part[:, (j * 4 + k) * 128:(j * 4 + k + 1) * 128].astype(BF16)
    cu = go(remote(s1u.at[1 - c], rcu, SEM["cu"], other_core))
    s3d[...] = sum_of_four(s2d[x], rxd, xd)
    zhd = to_three("zhd", lambda to: s3d.at[to], rhd, zh, "zh_")
    cu.wait_recv()
    s2u[...] = (s1u[c].astype(F32) + rcu[...].astype(F32)).astype(BF16)
    xu = to_three("xu", lambda to: s2u.at[to], rxu, x, "x_")
    s3u[...] = sum_of_four(s2u[x], rxu, xu)
    zhu = to_three("zhu", lambda to: s3u.at[to], rhu, zh, "zh_")
    s4d[...] = sum_of_four(s3d[zh], rhd, zhd)
    zld = to_three("zld", lambda to: s4d.at[div(to, 2)], rld, zl, "zl_")
    s4u[...] = sum_of_four(s3u[zh], rhu, zhu)
    zlu = to_three("zlu", lambda to: s4u, rlu, zl, "zl_")

    early = list(sent)
    last = []
    fd[y] = sum_of_four(s4d[div(zl, 2)], rld, zld)
    for k in (2, 1, 3):
        last.append(remote(fd.at[y], fd.at[y], SEM["xyd"] + k - 1, dev(y_=mod(y + k, 4))))
        last[-1].start()
    fu[y, x] = sum_of_four(s4u[...], rlu, zlu)
    for n, (i, j) in enumerate(plane):
        to = dev(y_=mod(y + i, 4), x_=mod(x + j, 4))
        last.append(remote(fu.at[y, x], fu.at[y, x], SEM["xyu"] + n, to))
        last[-1].start()

    for copy in early:
        copy.wait_send()
    for i in range(KV):
        dkv_copies[i].wait_recv()
        at = slice(i * HEAD, (i + 1) * HEAD)
        kg_v[0, :, at] = (dkv_own[i, 0] + dkv_in[i, 0].astype(F32)).astype(BF16)
        vg_v[0, :, at] = (dkv_own[i, 1] + dkv_in[i, 1].astype(F32)).astype(BF16)
    results = [local(kg_v, kg_o, L_OUT), local(vg_v, vg_o, L_OUT + 1)]
    for copy in results:
        copy.start()

    for copy in last + tens:
        copy.wait_recv()
    odd = jnp.broadcast_to(mod(zl, 2), (R, 64)) > 0
    for a in range(TEN):
        down = jnp.zeros((R, 128), F32)
        for j in range(4):
            down += jnp.where(ten_v[j].astype(F32) == a, fd[j].astype(F32), 0.0)
        down_v[a] = jnp.where(odd, down[:, 64:], down[:, :64])
        for k in range(4):
            up = jnp.zeros((R, 128), F32)
            for j in range(4):
                up += jnp.where(ten_v[j].astype(F32) == a, fu[j, k].astype(F32), 0.0)
            up_v[a, :, k * 128:(k + 1) * 128] = up

    results += [local(down_v, down_o, L_OUT + 2), local(up_v, up_o, L_OUT + 3)]
    for copy in results[2:]:
        copy.start()
    for copy in last:
        copy.wait_send()
    for copy in results:
        copy.wait()


def hand_over(*refs):
    given, taken, held, sems = refs[:4], refs[4:8], refs[8:12], refs[12]
    inward = [pltpu.make_async_copy(given[i], held[i], sems.at[0, i]) for i in range(4)]
    outward = [pltpu.make_async_copy(held[i], taken[i], sems.at[1, i]) for i in range(4)]
    for copy in inward:
        copy.start()
    for before, after in zip(inward, outward):
        before.wait()
        after.start()
    for copy in outward:
        copy.wait()


def local(queries, keys, values, output_gradient, layer_input, saved_log_total, row_dot_products, segment_ids, tenants,
          adapter_down, adapter_up):
    anywhere = pl.BlockSpec(memory_space=pl.ANY)
    results = (
        jax.ShapeDtypeStruct((1, TOK, KV * HEAD), BF16),
        jax.ShapeDtypeStruct((1, TOK, KV * HEAD), BF16),
        jax.ShapeDtypeStruct((TEN, R, 64), F32),
        jax.ShapeDtypeStruct((TEN, R, 512), F32),
    )
    raw = pl.pallas_call(
        kernel,
        out_shape=results,
        in_specs=[pl.BlockSpec(memory_space=pltpu.SMEM)] + [anywhere] * 10,
        out_specs=(anywhere,) * 4,
        scratch_shapes=[
            pltpu.VMEM((TOK, WIDE), BF16),
            pltpu.VMEM((TOK, WIDE), BF16),
            pltpu.VMEM((TOK, D), BF16),
            pltpu.VMEM((KV, 2, TOK, HEAD), BF16),
            pltpu.VMEM((KV, 2, TOK, HEAD), BF16),
            pltpu.VMEM((2, 4, 1024), F32),
            pltpu.VMEM((8, 2, 4, TOK), F32),
            pltpu.VMEM((2, 1, TOK), jnp.int32),
            pltpu.VMEM((TEN, R, 64), BF16),
            pltpu.VMEM((TEN, R, 512), BF16),
            pltpu.VMEM((2 * TOK, TOK), F32),
            pltpu.VMEM((KV, 2, TOK, HEAD), F32),
            pltpu.VMEM((KV, 2, TOK, HEAD), BF16),
            pltpu.VMEM((KV, 2, TOK, HEAD), BF16),
            pltpu.VMEM((WIDE, TOK), BF16),
            pltpu.VMEM((8, 2, R, 128), BF16),
            pltpu.VMEM((4, 4, 4, R, 128), BF16),
            pltpu.VMEM((4, 8, R, 128), BF16),
            pltpu.VMEM((4, R, 128), BF16),
            pltpu.VMEM((2, 4, 4, R, 128), BF16),
            pltpu.VMEM((2, 4, 4, 2, R, 128), BF16),
            pltpu.VMEM((4, 4, R, 128), BF16),
            pltpu.VMEM((4, 4, 2, R, 128), BF16),
            pltpu.VMEM((4, 4, R, 128), BF16),
            pltpu.VMEM((4, 4, 2, R, 128), BF16),
            pltpu.VMEM((3, 4, R, 128), BF16),
            pltpu.VMEM((3, 4, 2, R, 128), BF16),
            pltpu.VMEM((4, R, 128), BF16),
            pltpu.VMEM((4, 2, R, 128), BF16),
            pltpu.VMEM((3, R, 128), BF16),
            pltpu.VMEM((3, 2, R, 128), BF16),
            pltpu.VMEM((R, 128), BF16),
            pltpu.VMEM((2, R, 128), BF16),
            pltpu.VMEM((3, R, 128), BF16),
            pltpu.VMEM((3, R, 128), BF16),
            pltpu.VMEM((4, 4, R, 128), BF16),
            pltpu.VMEM((4, R, 128), BF16),
            pltpu.VMEM((1, TOK, KV * HEAD), BF16),
            pltpu.VMEM((1, TOK, KV * HEAD), BF16),
            pltpu.VMEM((TEN, R, 64), F32),
            pltpu.VMEM((TEN, R, 512), F32),
            pltpu.SemaphoreType.DMA((N_LOC,)),
            pltpu.SemaphoreType.DMA((N_SEM,)),
            pltpu.SemaphoreType.DMA((N_SEM,)),
        ],
        compiler_params=pltpu.CompilerParams(
            collective_id=0, has_side_effects=True, vmem_limit_bytes=60 * 1024 * 1024
        ),
        cost_estimate=pl.CostEstimate(flops=1_500_000_000, bytes_accessed=5_000_000, transcendentals=1_048_576),
    )(
        tenants, queries, keys, values, output_gradient, layer_input, saved_log_total, row_dot_products, segment_ids,
        jnp.swapaxes(adapter_down, 1, 2), adapter_up,
    )
    key_grad, value_grad, down_grad, up_grad = pl.pallas_call(
        hand_over,
        out_shape=results,
        in_specs=[anywhere] * 4,
        out_specs=(anywhere,) * 4,
        scratch_shapes=[pltpu.VMEM(r.shape, r.dtype) for r in results] + [pltpu.SemaphoreType.DMA((2, 4))],
        compiler_params=pltpu.CompilerParams(vmem_limit_bytes=60 * 1024 * 1024),
        cost_estimate=pl.CostEstimate(flops=0, bytes_accessed=1_000_000, transcendentals=0),
    )(*raw)
    return key_grad, value_grad, jnp.swapaxes(down_grad, 1, 2), up_grad


def solution(mesh):
    tokens = P("dp", ("blk", "uly"), None)
    rows = P("dp", "uly", "blk")
    return jax.shard_map(
        local,
        mesh=mesh,
        in_specs=(
            tokens, tokens, tokens, tokens, tokens, rows, rows, P("dp", None), P("dp"),
            P(None, ("blk", "uly"), None), P(None, None, "uly"),
        ),
        out_specs=(tokens, tokens, P(None, ("blk", "uly"), None), P(None, None, "uly")),
        check_vma=False,
    )
```

```python
import jax
import jax.numpy as jnp
from jax import lax
from jax.experimental import pallas as pl
from jax.experimental.pallas import tpu as pltpu
from jax.sharding import PartitionSpec as P

MESH = pl.DeviceIdType.MESH
F32 = jnp.float32
BF16 = jnp.bfloat16

HEAD = 128
HEADS = 32
KV = 4
GROUP = HEADS // KV
TEN = 4
R = 16
TOK = 128
D = 8192
SEQ = 16384
WIDE = HEADS * HEAD
SCALE = HEAD ** -0.5
LOG2E = 1.4426950408889634
ADAPTER_SCALE = 2.0
NT = (((1,), (1,)), ((), ()))
NN = (((1,), (0,)), ((), ()))
TN = (((0,), (0,)), ((), ()))


def dot(a, b, dims):
    return lax.dot_general(a, b, dims, preferred_element_type=F32)


def mod(a, n):
    return lax.rem(a, jnp.int32(n))


def div(a, n):
    return lax.div(a, jnp.int32(n))


class Sems:
    def __init__(self):
        self.count = 0

    def take(self, n):
        first = self.count
        self.count += n
        return first


def layout():
    s = Sems()
    names = dict(
        ld=7, kv=4, dkv=4, au=7, ten=3, a2=15, u3=3, cu=1, cd=1, xu=3, xd=3,
        zhu=3, zhd=3, zlu=3, zld=3, xyu=15, xyd=3,
    )
    return {name: s.take(n) for name, n in names.items()}, s.count


SEM, N_SEM = layout()
L_KV, L_LD, L_SEG, L_ADN, L_AUP, L_Q, L_G, L_X, L_OUT, N_LOC = 0, 8, 10, 12, 13, 14, 15, 16, 17, 21


def kernel(
    ten_s, q_h, k_h, v_h, g_h, x_h, lse_h, dots_h, seg_h, adn_h, aup_h,
    kg_o, vg_o, down_o, up_o,
    q_v, g_v, x_v, kv_v, halo, ld_v, ld_all, seg_v, adn_v, aup_v, bias_v,
    dkv_own, dkv_out, dkv_in, dqt, au, ag, ug, ten_v,
    s1u, s1d, rcu, rcd, s2u, s2d, rxu, rxd, s3u, s3d, rhu, rhd, s4u, s4d, rlu, rld, fu, fd, kg_v, vg_v, down_v, up_v,
    loc, ssem, rsem,
):
    y = lax.axis_index("dp")
    b = lax.axis_index("blk")
    u = lax.axis_index("uly")
    zl, x = div(b, 4), mod(b, 4)
    zh, c = div(u, 2), mod(u, 2)
    t = b * 8 + u

    def dev(y_=y, zl_=zl, x_=x, zh_=zh, c_=c):
        return (y_, zl_ * 4 + x_, zh_ * 2 + c_)

    def token_dev(t_):
        return (y, div(t_, 8), mod(t_, 8))

    following = token_dev(mod(t + 1, 128))
    previous = token_dev(mod(t + 127, 128))

    def local(src, dst, i):
        return pltpu.make_async_copy(src, dst, loc.at[i])

    def remote(src, dst, i, to):
        return pltpu.make_async_remote_copy(
            src_ref=src, dst_ref=dst, send_sem=ssem.at[i], recv_sem=rsem.at[i], device_id=to, device_id_type=MESH
        )

    peers = [previous, following]
    peers += [dev(zh_=mod(zh + k, 4)) for k in (1, 2, 3)]
    peers += [dev(zh_=mod(zh + k, 4), c_=1 - c) for k in (0, 1, 2, 3)]
    plane = [(i, j) for i in range(4) for j in range(4) if (i, j) != (0, 0)]
    peers += [dev(zl_=mod(zl + i, 4), x_=mod(x + j, 4)) for i, j in plane]
    peers += [dev(y_=mod(y + i, 4), x_=mod(x + j, 4)) for i, j in plane if i != 0]
    barrier = pltpu.get_barrier_semaphore()
    for to in peers:
        pl.semaphore_signal(barrier, inc=1, device_id=to, device_id_type=MESH)

    small = [
        local(adn_h, adn_v, L_ADN),
        local(aup_h, aup_v, L_AUP),
        local(lse_h.at[0], ld_v.at[0], L_LD),
        local(dots_h.at[0], ld_v.at[1], L_LD + 1),
        local(seg_h.at[:, pl.ds(pl.multiple_of(t * TOK, TOK), TOK)], seg_v.at[1], L_SEG),
        local(seg_h.at[:, pl.ds(pl.multiple_of(mod(t + 127, 128) * TOK, TOK), TOK)], seg_v.at[0], L_SEG + 1),
    ]
    kv_loads = []
    for i in range(KV):
        kv_loads.append(local(k_h.at[0, :, pl.ds(i * HEAD, HEAD)], kv_v.at[i, 0], L_KV + 2 * i))
        kv_loads.append(local(v_h.at[0, :, pl.ds(i * HEAD, HEAD)], kv_v.at[i, 1], L_KV + 2 * i + 1))
    big = [local(q_h.at[0], q_v, L_Q), local(g_h.at[0], g_v, L_G)]
    x_load = local(x_h.at[0], x_v, L_X)
    for copy in small + kv_loads + big + [x_load]:
        copy.start()

    for copy in small:
        copy.wait()
    tenant = jnp.full((R, 128), ten_s[0], jnp.int32)
    ten_v[y] = tenant.astype(F32).astype(BF16)
    down_sel = jnp.zeros((R, 64), F32)
    up_sel = jnp.zeros((R, 128), F32)
    for a in range(TEN):
        down_sel += jnp.where(tenant[:, :64] == a, adn_v[a].astype(F32), 0.0)
        up_sel += jnp.where(tenant == a, aup_v[a, :, pl.ds(pl.multiple_of(x * 128, 128), 128)].astype(F32), 0.0)
    place = lax.broadcasted_iota(jnp.int32, (64, 128), 1) - lax.broadcasted_iota(jnp.int32, (64, 128), 0)
    shift = jnp.where(place == c * 64, 1.0, 0.0).astype(BF16)
    au[u, 0] = dot(down_sel.astype(BF16), shift, NN).astype(BF16)
    au[u, 1] = up_sel.astype(BF16)
    ld_all[u] = ld_v[:, :, pl.ds(pl.multiple_of(u * TOK, TOK), TOK)]
    row = lax.broadcasted_iota(jnp.int32, (TOK, TOK), 0)
    col = lax.broadcasted_iota(jnp.int32, (TOK, TOK), 1)
    ids_now = jnp.broadcast_to(seg_v[1].astype(F32), (TOK, TOK))
    ids_before = jnp.broadcast_to(seg_v[0].astype(F32), (TOK, TOK))
    now_rows = jnp.sum(jnp.where(row == col, ids_now, 0.0), axis=1, keepdims=True)
    before_rows = jnp.sum(jnp.where(row == col, ids_before, 0.0), axis=1, keepdims=True)
    first = jnp.broadcast_to(t, (TOK, TOK)) > 0
    bias_v[:TOK] = jnp.where((row > col) & (before_rows == ids_now) & first, 0.0, -1e30)
    bias_v[TOK:] = jnp.where((row <= col) & (now_rows == ids_now), 0.0, -1e30)

    for copy in kv_loads:
        copy.wait()
    pl.semaphore_wait(barrier, len(peers))

    sent = []

    def go(copy):
        copy.start()
        sent.append(copy)
        return copy

    other_core = dev(c_=1 - c)
    au_copies, ld_copies = [], []
    others = [(k, other) for k in (2, 1, 3, 0) for other in (0, 1) if (k, other) != (0, 0)]
    for n, (k, other) in enumerate(others):
        to = dev(zh_=mod(zh + k, 4), c_=(1 - c) if other else c)
        au_copies.append(go(remote(au.at[u], au.at[u], SEM["au"] + n, to)))
    for n, (k, other) in enumerate(others):
        zh_to = mod(zh + k, 4)
        c_to = (1 - c) if other else c
        piece = pl.ds(pl.multiple_of((zh_to * 2 + c_to) * TOK, TOK), TOK)
        ld_copies.append(go(remote(ld_v.at[:, :, piece], ld_all.at[u], SEM["ld"] + n, dev(zh_=zh_to, c_=c_to))))
    kv_copies = [go(remote(kv_v.at[i], halo.at[i], SEM["kv"] + i, following)) for i in range(KV)]
    tens = [
        go(remote(ten_v.at[y], ten_v.at[y], SEM["ten"] + k - 1, dev(y_=mod(y + k, 4)))) for k in (1, 2, 3)
    ]

    for copy in au_copies:
        copy.wait_recv()
    for j in range(4):
        ag[zl, x, j] = au[2 * j, 0] + au[2 * j + 1, 0]
    for j in range(8):
        ug[x, j] = au[j, 1]
    a2 = []
    for n, (i, j) in enumerate(plane):
        to = dev(zl_=mod(zl + i, 4), x_=mod(x + j, 4))
        a2.append(go(remote(ag.at[zl, x], ag.at[zl, x], SEM["a2"] + n, to)))
    u3 = [go(remote(ug.at[x], ug.at[x], SEM["u3"] + k - 1, dev(x_=mod(x + k, 4)))) for k in (1, 2, 3)]
    for copy in big:
        copy.wait()
    for copy in ld_copies:
        copy.wait_recv()

    def one_head(i):
        keys = jnp.concatenate([halo[i, 0], kv_v[i, 0]], axis=0)
        values = jnp.concatenate([halo[i, 1], kv_v[i, 1]], axis=0)
        q_list, g_list, p_list, s_list = [], [], [], []
        for half in range(2):
            heads = range(half * 4, half * 4 + 4)
            q = jnp.concatenate([q_v[:, (i * GROUP + h) * HEAD:(i * GROUP + h + 1) * HEAD] for h in heads], axis=0)
            g = jnp.concatenate([g_v[:, (i * GROUP + h) * HEAD:(i * GROUP + h + 1) * HEAD] for h in heads], axis=0)
            scores = dot(keys, q, NT)
            grads = dot(values, g, NT)
            q_list.append(q)
            g_list.append(g)
            for n in range(4):
                at = slice(n * TOK, (n + 1) * TOK)
                lse = ld_all[2 * i + half, 0, n:n + 1] * LOG2E
                dots = ld_all[2 * i + half, 1, n:n + 1]
                probs = jnp.exp2((scores[:, at] * (SCALE * LOG2E) - lse) + bias_v[...])
                p_list.append(probs.astype(BF16))
                s_list.append((probs * (grads[:, at] - dots)).astype(BF16))
        score_grad = jnp.concatenate(s_list, axis=1)
        value_part = dot(jnp.concatenate(p_list, axis=1), jnp.concatenate(g_list, axis=0), NN)
        key_part = dot(score_grad, jnp.concatenate(q_list, axis=0), NN) * SCALE
        query_part = (dot(keys, score_grad, TN) * SCALE).astype(BF16)
        dkv_out[i, 0] = key_part[:TOK].astype(BF16)
        dkv_out[i, 1] = value_part[:TOK].astype(BF16)
        dkv_own[i, 0] = key_part[TOK:]
        dkv_own[i, 1] = value_part[TOK:]
        for h in range(GROUP):
            dqt[(i * GROUP + h) * HEAD:(i * GROUP + h + 1) * HEAD] = query_part[:, h * HEAD:(h + 1) * HEAD]

    dkv_copies = [remote(dkv_out.at[i], dkv_in.at[i], SEM["dkv"] + i, previous) for i in range(KV)]

    for i in range(KV):
        kv_copies[i].wait_recv()
        one_head(i)
        if i < 2:
            go(dkv_copies[i])

    for copy in u3:
        copy.wait_recv()
    x_load.wait()

    def to_three(name, source, target, place, axis):
        copies = []
        for k in (2, 1, 3):
            to = mod(place + k, 4)
            copies.append(go(remote(source(to), target.at[k - 1], SEM[name] + k - 1, dev(**{axis: to}))))
        return copies

    def sum_of_four(own, target, copies):
        total = own.astype(F32)
        for k, copy in zip((2, 1, 3), copies):
            copy.wait_recv()
            total += target[k - 1].astype(F32)
        return total.astype(BF16)

    up_rows = jnp.concatenate([ug[k, n] for n in range(8) for k in range(4)], axis=1)
    coeff = (ADAPTER_SCALE * dot(up_rows, dqt[...], NN)).astype(BF16)
    left = lax.broadcasted_iota(jnp.int32, (R, 128), 1) < 64
    for m in range(2):
        part = dot(coeff, x_v[:, m * 4096:(m + 1) * 4096], NN)
        for n in range(4):
            for j in range(4):
                a = part[:, (n * 4 + j) * 128:(n * 4 + j + 1) * 128]
                d = part[:, 2048 + (n * 4 + j) * 128:2048 + (n * 4 + j + 1) * 128]
                s1d[0, n, j, m] = jnp.where(left, a, pltpu.roll(d, 64, 1)).astype(BF16)
                s1d[1, n, j, m] = jnp.where(left, pltpu.roll(a, 64, 1), d).astype(BF16)
    cd = go(remote(s1d.at[1 - c], rcd, SEM["cd"], other_core))

    for copy in a2:
        copy.wait_recv()
    down_rows = jnp.concatenate([ag[i, j, k] for i in range(4) for j in range(4) for k in range(4)], axis=1)
    low = (ADAPTER_SCALE * dot(down_rows, x_v[...], NT).astype(BF16).astype(F32)).astype(BF16)
    for n in range(KV):
        part = dot(low, dqt[n * 1024:(n + 1) * 1024], NT)
        for j in range(2):
            for k in range(4):
                s1u[j, k, n] = part[:, (j * 4 + k) * 128:(j * 4 + k + 1) * 128].astype(BF16)
    cu = go(remote(s1u.at[1 - c], rcu, SEM["cu"], other_core))

    cd.wait_recv()
    s2d[...] = (s1d[c].astype(F32) + rcd[...].astype(F32)).astype(BF16)
    xd = to_three("xd", lambda to: s2d.at[to], rxd, x, "x_")
    cu.wait_recv()
    s2u[...] = (s1u[c].astype(F32) + rcu[...].astype(F32)).astype(BF16)
    xu = to_three("xu", lambda to: s2u.at[to], rxu, x, "x_")
    go(dkv_copies[2])
    s3d[...] = sum_of_four(s2d[x], rxd, xd)
    zhd = to_three("zhd", lambda to: s3d.at[to], rhd, zh, "zh_")
    s3u[...] = sum_of_four(s2u[x], rxu, xu)
    zhu = to_three("zhu", lambda to: s3u.at[to], rhu, zh, "zh_")
    go(dkv_copies[3])
    s4d[...] = sum_of_four(s3d[zh], rhd, zhd)
    zld = to_three("zld", lambda to: s4d.at[div(to, 2)], rld, zl, "zl_")
    s4u[...] = sum_of_four(s3u[zh], rhu, zhu)
    zlu = to_three("zlu", lambda to: s4u, rlu, zl, "zl_")

    early = list(sent)
    last = []
    fd[y] = sum_of_four(s4d[div(zl, 2)], rld, zld)
    for k in (2, 1, 3):
        last.append(remote(fd.at[y], fd.at[y], SEM["xyd"] + k - 1, dev(y_=mod(y + k, 4))))
        last[-1].start()
    fu[y, x] = sum_of_four(s4u[...], rlu, zlu)
    for n, (i, j) in enumerate(plane):
        to = dev(y_=mod(y + i, 4), x_=mod(x + j, 4))
        last.append(remote(fu.at[y, x], fu.at[y, x], SEM["xyu"] + n, to))
        last[-1].start()

    for copy in early:
        copy.wait_send()
    for i in range(KV):
        dkv_copies[i].wait_recv()
        at = slice(i * HEAD, (i + 1) * HEAD)
        kg_v[0, :, at] = (dkv_own[i, 0] + dkv_in[i, 0].astype(F32)).astype(BF16)
        vg_v[0, :, at] = (dkv_own[i, 1] + dkv_in[i, 1].astype(F32)).astype(BF16)
    results = [local(kg_v, kg_o, L_OUT), local(vg_v, vg_o, L_OUT + 1)]
    for copy in results:
        copy.start()

    for copy in last + tens:
        copy.wait_recv()
    odd = jnp.broadcast_to(mod(zl, 2), (R, 64)) > 0
    for a in range(TEN):
        down = jnp.zeros((R, 128), F32)
        for j in range(4):
            down += jnp.where(ten_v[j].astype(F32) == a, fd[j].astype(F32), 0.0)
        down_v[a] = jnp.where(odd, down[:, 64:], down[:, :64])
        for k in range(4):
            up = jnp.zeros((R, 128), F32)
            for j in range(4):
                up += jnp.where(ten_v[j].astype(F32) == a, fu[j, k].astype(F32), 0.0)
            up_v[a, :, k * 128:(k + 1) * 128] = up

    results += [local(down_v, down_o, L_OUT + 2), local(up_v, up_o, L_OUT + 3)]
    for copy in results[2:]:
        copy.start()
    for copy in last:
        copy.wait_send()
    for copy in results:
        copy.wait()


def hand_over(*refs):
    given, taken, held, sems = refs[:4], refs[4:8], refs[8:12], refs[12]
    inward = [pltpu.make_async_copy(given[i], held[i], sems.at[0, i]) for i in range(4)]
    outward = [pltpu.make_async_copy(held[i], taken[i], sems.at[1, i]) for i in range(4)]
    for copy in inward:
        copy.start()
    for before, after in zip(inward, outward):
        before.wait()
        after.start()
    for copy in outward:
        copy.wait()


def local(queries, keys, values, output_gradient, layer_input, saved_log_total, row_dot_products, segment_ids, tenants,
          adapter_down, adapter_up):
    anywhere = pl.BlockSpec(memory_space=pl.ANY)
    results = (
        jax.ShapeDtypeStruct((1, TOK, KV * HEAD), BF16),
        jax.ShapeDtypeStruct((1, TOK, KV * HEAD), BF16),
        jax.ShapeDtypeStruct((TEN, R, 64), F32),
        jax.ShapeDtypeStruct((TEN, R, 512), F32),
    )
    raw = pl.pallas_call(
        kernel,
        out_shape=results,
        in_specs=[pl.BlockSpec(memory_space=pltpu.SMEM)] + [anywhere] * 10,
        out_specs=(anywhere,) * 4,
        scratch_shapes=[
            pltpu.VMEM((TOK, WIDE), BF16),
            pltpu.VMEM((TOK, WIDE), BF16),
            pltpu.VMEM((TOK, D), BF16),
            pltpu.VMEM((KV, 2, TOK, HEAD), BF16),
            pltpu.VMEM((KV, 2, TOK, HEAD), BF16),
            pltpu.VMEM((2, 4, 1024), F32),
            pltpu.VMEM((8, 2, 4, TOK), F32),
            pltpu.VMEM((2, 1, TOK), jnp.int32),
            pltpu.VMEM((TEN, R, 64), BF16),
            pltpu.VMEM((TEN, R, 512), BF16),
            pltpu.VMEM((2 * TOK, TOK), F32),
            pltpu.VMEM((KV, 2, TOK, HEAD), F32),
            pltpu.VMEM((KV, 2, TOK, HEAD), BF16),
            pltpu.VMEM((KV, 2, TOK, HEAD), BF16),
            pltpu.VMEM((WIDE, TOK), BF16),
            pltpu.VMEM((8, 2, R, 128), BF16),
            pltpu.VMEM((4, 4, 4, R, 128), BF16),
            pltpu.VMEM((4, 8, R, 128), BF16),
            pltpu.VMEM((4, R, 128), BF16),
            pltpu.VMEM((2, 4, 4, R, 128), BF16),
            pltpu.VMEM((2, 4, 4, 2, R, 128), BF16),
            pltpu.VMEM((4, 4, R, 128), BF16),
            pltpu.VMEM((4, 4, 2, R, 128), BF16),
            pltpu.VMEM((4, 4, R, 128), BF16),
            pltpu.VMEM((4, 4, 2, R, 128), BF16),
            pltpu.VMEM((3, 4, R, 128), BF16),
            pltpu.VMEM((3, 4, 2, R, 128), BF16),
            pltpu.VMEM((4, R, 128), BF16),
            pltpu.VMEM((4, 2, R, 128), BF16),
            pltpu.VMEM((3, R, 128), BF16),
            pltpu.VMEM((3, 2, R, 128), BF16),
            pltpu.VMEM((R, 128), BF16),
            pltpu.VMEM((2, R, 128), BF16),
            pltpu.VMEM((3, R, 128), BF16),
            pltpu.VMEM((3, R, 128), BF16),
            pltpu.VMEM((4, 4, R, 128), BF16),
            pltpu.VMEM((4, R, 128), BF16),
            pltpu.VMEM((1, TOK, KV * HEAD), BF16),
            pltpu.VMEM((1, TOK, KV * HEAD), BF16),
            pltpu.VMEM((TEN, R, 64), F32),
            pltpu.VMEM((TEN, R, 512), F32),
            pltpu.SemaphoreType.DMA((N_LOC,)),
            pltpu.SemaphoreType.DMA((N_SEM,)),
            pltpu.SemaphoreType.DMA((N_SEM,)),
        ],
        compiler_params=pltpu.CompilerParams(
            collective_id=0, has_side_effects=True, vmem_limit_bytes=60 * 1024 * 1024
        ),
        cost_estimate=pl.CostEstimate(flops=1_500_000_000, bytes_accessed=5_000_000, transcendentals=1_048_576),
    )(
        tenants, queries, keys, values, output_gradient, layer_input, saved_log_total, row_dot_products, segment_ids,
        jnp.swapaxes(adapter_down, 1, 2), adapter_up,
    )
    key_grad, value_grad, down_grad, up_grad = pl.pallas_call(
        hand_over,
        out_shape=results,
        in_specs=[anywhere] * 4,
        out_specs=(anywhere,) * 4,
        scratch_shapes=[pltpu.VMEM(r.shape, r.dtype) for r in results] + [pltpu.SemaphoreType.DMA((2, 4))],
        compiler_params=pltpu.CompilerParams(vmem_limit_bytes=60 * 1024 * 1024),
        cost_estimate=pl.CostEstimate(flops=0, bytes_accessed=1_000_000, transcendentals=0),
    )(*raw)
    return key_grad, value_grad, jnp.swapaxes(down_grad, 1, 2), up_grad


def solution(mesh):
    tokens = P("dp", ("blk", "uly"), None)
    rows = P("dp", "uly", "blk")
    return jax.shard_map(
        local,
        mesh=mesh,
        in_specs=(
            tokens, tokens, tokens, tokens, tokens, rows, rows, P("dp", None), P("dp"),
            P(None, ("blk", "uly"), None), P(None, None, "uly"),
        ),
        out_specs=(tokens, tokens, P(None, ("blk", "uly"), None), P(None, None, "uly")),
        check_vma=False,
    )
```

```python
import jax
import jax.numpy as jnp
from jax import lax
from jax.experimental import pallas as pl
from jax.experimental.pallas import tpu as pltpu
from jax.sharding import PartitionSpec as P

MESH = pl.DeviceIdType.MESH
F32 = jnp.float32
BF16 = jnp.bfloat16

HEAD = 128
HEADS = 32
KV = 4
GROUP = HEADS // KV
TEN = 4
R = 16
TOK = 128
D = 8192
SEQ = 16384
WIDE = HEADS * HEAD
SCALE = HEAD ** -0.5
LOG2E = 1.4426950408889634
ADAPTER_SCALE = 2.0
NT = (((1,), (1,)), ((), ()))
NN = (((1,), (0,)), ((), ()))
TN = (((0,), (0,)), ((), ()))


def dot(a, b, dims):
    return lax.dot_general(a, b, dims, preferred_element_type=F32)


def mod(a, n):
    return lax.rem(a, jnp.int32(n))


def div(a, n):
    return lax.div(a, jnp.int32(n))


class Sems:
    def __init__(self):
        self.count = 0

    def take(self, n):
        first = self.count
        self.count += n
        return first


def layout():
    s = Sems()
    names = dict(
        ld=7, kv=4, dkv=4, au=7, ten=3, a2=15, u3=3, cu=1, cd=1, xu=3, xd=3,
        zhu=3, zhd=3, zlu=3, zld=3, xyu=15, xyd=3,
    )
    return {name: s.take(n) for name, n in names.items()}, s.count


SEM, N_SEM = layout()
L_KV, L_LD, L_SEG, L_ADN, L_AUP, L_Q, L_G, L_X, L_OUT, N_LOC = 0, 8, 10, 12, 13, 14, 15, 16, 17, 21


def kernel(
    ten_s, q_h, k_h, v_h, g_h, x_h, lse_h, dots_h, seg_h, adn_h, aup_h,
    kg_o, vg_o, down_o, up_o,
    q_v, g_v, x_v, kv_v, halo, ld_v, ld_all, seg_v, adn_v, aup_v, bias_v,
    dkv_own, dkv_out, dkv_in, dqt, au, ag, ug, ten_v,
    s1u, s1d, rcu, rcd, s2u, s2d, rxu, rxd, s3u, s3d, rhu, rhd, s4u, s4d, rlu, rld, fu, fd, kg_v, vg_v, down_v, up_v,
    loc, ssem, rsem,
):
    y = lax.axis_index("dp")
    b = lax.axis_index("blk")
    u = lax.axis_index("uly")
    zl, x = div(b, 4), mod(b, 4)
    zh, c = div(u, 2), mod(u, 2)
    t = b * 8 + u

    def dev(y_=y, zl_=zl, x_=x, zh_=zh, c_=c):
        return (y_, zl_ * 4 + x_, zh_ * 2 + c_)

    def token_dev(t_):
        return (y, div(t_, 8), mod(t_, 8))

    following = token_dev(mod(t + 1, 128))
    previous = token_dev(mod(t + 127, 128))

    def local(src, dst, i):
        return pltpu.make_async_copy(src, dst, loc.at[i])

    def remote(src, dst, i, to):
        return pltpu.make_async_remote_copy(
            src_ref=src, dst_ref=dst, send_sem=ssem.at[i], recv_sem=rsem.at[i], device_id=to, device_id_type=MESH
        )

    peers = [previous, following]
    peers += [dev(zh_=mod(zh + k, 4)) for k in (1, 2, 3)]
    peers += [dev(zh_=mod(zh + k, 4), c_=1 - c) for k in (0, 1, 2, 3)]
    plane = [(i, j) for i in range(4) for j in range(4) if (i, j) != (0, 0)]
    peers += [dev(zl_=mod(zl + i, 4), x_=mod(x + j, 4)) for i, j in plane]
    peers += [dev(y_=mod(y + i, 4), x_=mod(x + j, 4)) for i, j in plane if i != 0]
    barrier = pltpu.get_barrier_semaphore()
    for to in peers:
        pl.semaphore_signal(barrier, inc=1, device_id=to, device_id_type=MESH)

    small = [
        local(adn_h, adn_v, L_ADN),
        local(aup_h, aup_v, L_AUP),
        local(lse_h.at[0], ld_v.at[0], L_LD),
        local(dots_h.at[0], ld_v.at[1], L_LD + 1),
        local(seg_h.at[:, pl.ds(pl.multiple_of(t * TOK, TOK), TOK)], seg_v.at[1], L_SEG),
        local(seg_h.at[:, pl.ds(pl.multiple_of(mod(t + 127, 128) * TOK, TOK), TOK)], seg_v.at[0], L_SEG + 1),
    ]
    kv_loads = []
    for i in range(KV):
        kv_loads.append(local(k_h.at[0, :, pl.ds(i * HEAD, HEAD)], kv_v.at[i, 0], L_KV + 2 * i))
        kv_loads.append(local(v_h.at[0, :, pl.ds(i * HEAD, HEAD)], kv_v.at[i, 1], L_KV + 2 * i + 1))
    big = [local(q_h.at[0], q_v, L_Q), local(g_h.at[0], g_v, L_G)]
    x_load = local(x_h.at[0], x_v, L_X)
    for copy in small + kv_loads + big + [x_load]:
        copy.start()

    for copy in small:
        copy.wait()
    tenant = jnp.full((R, 128), ten_s[0], jnp.int32)
    ten_v[y] = tenant.astype(F32).astype(BF16)
    down_sel = jnp.zeros((R, 64), F32)
    up_sel = jnp.zeros((R, 128), F32)
    for a in range(TEN):
        down_sel += jnp.where(tenant[:, :64] == a, adn_v[a].astype(F32), 0.0)
        up_sel += jnp.where(tenant == a, aup_v[a, :, pl.ds(pl.multiple_of(x * 128, 128), 128)].astype(F32), 0.0)
    place = lax.broadcasted_iota(jnp.int32, (64, 128), 1) - lax.broadcasted_iota(jnp.int32, (64, 128), 0)
    shift = jnp.where(place == c * 64, 1.0, 0.0).astype(BF16)
    au[u, 0] = dot(down_sel.astype(BF16), shift, NN).astype(BF16)
    au[u, 1] = up_sel.astype(BF16)
    ld_all[u] = ld_v[:, :, pl.ds(pl.multiple_of(u * TOK, TOK), TOK)]
    for copy in kv_loads:
        copy.wait()
    pl.semaphore_wait(barrier, len(peers))

    sent = []

    def go(copy):
        copy.start()
        sent.append(copy)
        return copy

    other_core = dev(c_=1 - c)
    au_copies, ld_copies = [], []
    others = [(k, other) for k in (2, 1, 3, 0) for other in (0, 1) if (k, other) != (0, 0)]
    for n, (k, other) in enumerate(others):
        to = dev(zh_=mod(zh + k, 4), c_=(1 - c) if other else c)
        au_copies.append(go(remote(au.at[u], au.at[u], SEM["au"] + n, to)))
    for n, (k, other) in enumerate(others):
        zh_to = mod(zh + k, 4)
        c_to = (1 - c) if other else c
        piece = pl.ds(pl.multiple_of((zh_to * 2 + c_to) * TOK, TOK), TOK)
        ld_copies.append(go(remote(ld_v.at[:, :, piece], ld_all.at[u], SEM["ld"] + n, dev(zh_=zh_to, c_=c_to))))
    kv_copies = [go(remote(kv_v.at[i], halo.at[i], SEM["kv"] + i, following)) for i in range(KV)]
    tens = [
        go(remote(ten_v.at[y], ten_v.at[y], SEM["ten"] + k - 1, dev(y_=mod(y + k, 4)))) for k in (1, 2, 3)
    ]

    row = lax.broadcasted_iota(jnp.int32, (TOK, TOK), 0)
    col = lax.broadcasted_iota(jnp.int32, (TOK, TOK), 1)
    ids_now = jnp.broadcast_to(seg_v[1].astype(F32), (TOK, TOK))
    ids_before = jnp.broadcast_to(seg_v[0].astype(F32), (TOK, TOK))
    now_rows = jnp.sum(jnp.where(row == col, ids_now, 0.0), axis=1, keepdims=True)
    before_rows = jnp.sum(jnp.where(row == col, ids_before, 0.0), axis=1, keepdims=True)
    first = jnp.broadcast_to(t, (TOK, TOK)) > 0
    bias_v[:TOK] = jnp.where((row > col) & (before_rows == ids_now) & first, 0.0, -1e30)
    bias_v[TOK:] = jnp.where((row <= col) & (now_rows == ids_now), 0.0, -1e30)

    for copy in au_copies:
        copy.wait_recv()
    for j in range(4):
        ag[zl, x, j] = au[2 * j, 0] + au[2 * j + 1, 0]
    for j in range(8):
        ug[x, j] = au[j, 1]
    a2 = []
    for n, (i, j) in enumerate(plane):
        to = dev(zl_=mod(zl + i, 4), x_=mod(x + j, 4))
        a2.append(go(remote(ag.at[zl, x], ag.at[zl, x], SEM["a2"] + n, to)))
    u3 = [go(remote(ug.at[x], ug.at[x], SEM["u3"] + k - 1, dev(x_=mod(x + k, 4)))) for k in (1, 2, 3)]
    for copy in big:
        copy.wait()
    for copy in ld_copies:
        copy.wait_recv()

    def one_head(i):
        keys = jnp.concatenate([halo[i, 0], kv_v[i, 0]], axis=0)
        values = jnp.concatenate([halo[i, 1], kv_v[i, 1]], axis=0)
        q_list, g_list, p_list, s_list = [], [], [], []
        for half in range(2):
            heads = range(half * 4, half * 4 + 4)
            q = jnp.concatenate([q_v[:, (i * GROUP + h) * HEAD:(i * GROUP + h + 1) * HEAD] for h in heads], axis=0)
            g = jnp.concatenate([g_v[:, (i * GROUP + h) * HEAD:(i * GROUP + h + 1) * HEAD] for h in heads], axis=0)
            scores = dot(keys, q, NT)
            grads = dot(values, g, NT)
            q_list.append(q)
            g_list.append(g)
            for n in range(4):
                at = slice(n * TOK, (n + 1) * TOK)
                lse = ld_all[2 * i + half, 0, n:n + 1] * LOG2E
                dots = ld_all[2 * i + half, 1, n:n + 1]
                probs = jnp.exp2((scores[:, at] * (SCALE * LOG2E) - lse) + bias_v[...])
                p_list.append(probs.astype(BF16))
                s_list.append((probs * (grads[:, at] - dots)).astype(BF16))
        score_grad = jnp.concatenate(s_list, axis=1)
        value_part = dot(jnp.concatenate(p_list, axis=1), jnp.concatenate(g_list, axis=0), NN)
        key_part = dot(score_grad, jnp.concatenate(q_list, axis=0), NN) * SCALE
        query_part = (dot(keys, score_grad, TN) * SCALE).astype(BF16)
        dkv_out[i, 0] = key_part[:TOK].astype(BF16)
        dkv_out[i, 1] = value_part[:TOK].astype(BF16)
        dkv_own[i, 0] = key_part[TOK:]
        dkv_own[i, 1] = value_part[TOK:]
        for h in range(GROUP):
            dqt[(i * GROUP + h) * HEAD:(i * GROUP + h + 1) * HEAD] = query_part[:, h * HEAD:(h + 1) * HEAD]

    dkv_copies = [remote(dkv_out.at[i], dkv_in.at[i], SEM["dkv"] + i, previous) for i in range(KV)]

    for i in range(KV):
        kv_copies[i].wait_recv()
        one_head(i)
        if i < 2:
            go(dkv_copies[i])

    for copy in u3:
        copy.wait_recv()
    x_load.wait()

    def to_three(name, source, target, place, axis):
        copies = []
        for k in (2, 1, 3):
            to = mod(place + k, 4)
            copies.append(go(remote(source(to), target.at[k - 1], SEM[name] + k - 1, dev(**{axis: to}))))
        return copies

    def sum_of_four(own, target, copies):
        total = own.astype(F32)
        for k, copy in zip((2, 1, 3), copies):
            copy.wait_recv()
            total += target[k - 1].astype(F32)
        return total.astype(BF16)

    up_rows = jnp.concatenate([ug[k, n] for n in range(8) for k in range(4)], axis=1)
    coeff = (ADAPTER_SCALE * dot(up_rows, dqt[...], NN)).astype(BF16)
    left = lax.broadcasted_iota(jnp.int32, (R, 128), 1) < 64
    for m in range(2):
        part = dot(coeff, x_v[:, m * 4096:(m + 1) * 4096], NN)
        for n in range(4):
            for j in range(4):
                a = part[:, (n * 4 + j) * 128:(n * 4 + j + 1) * 128]
                d = part[:, 2048 + (n * 4 + j) * 128:2048 + (n * 4 + j + 1) * 128]
                s1d[0, n, j, m] = jnp.where(left, a, pltpu.roll(d, 64, 1)).astype(BF16)
                s1d[1, n, j, m] = jnp.where(left, pltpu.roll(a, 64, 1), d).astype(BF16)
    cd = go(remote(s1d.at[1 - c], rcd, SEM["cd"], other_core))

    for copy in a2:
        copy.wait_recv()
    down_rows = jnp.concatenate([ag[i, j, k] for i in range(4) for j in range(4) for k in range(4)], axis=1)
    low = (ADAPTER_SCALE * dot(down_rows, x_v[...], NT).astype(BF16).astype(F32)).astype(BF16)
    for n in range(KV):
        part = dot(low, dqt[n * 1024:(n + 1) * 1024], NT)
        for j in range(2):
            for k in range(4):
                s1u[j, k, n] = part[:, (j * 4 + k) * 128:(j * 4 + k + 1) * 128].astype(BF16)
    cu = go(remote(s1u.at[1 - c], rcu, SEM["cu"], other_core))

    cd.wait_recv()
    s2d[...] = (s1d[c].astype(F32) + rcd[...].astype(F32)).astype(BF16)
    xd = to_three("xd", lambda to: s2d.at[to], rxd, x, "x_")
    cu.wait_recv()
    s2u[...] = (s1u[c].astype(F32) + rcu[...].astype(F32)).astype(BF16)
    xu = to_three("xu", lambda to: s2u.at[to], rxu, x, "x_")
    go(dkv_copies[2])
    s3d[...] = sum_of_four(s2d[x], rxd, xd)
    zhd = to_three("zhd", lambda to: s3d.at[to], rhd, zh, "zh_")
    s3u[...] = sum_of_four(s2u[x], rxu, xu)
    zhu = to_three("zhu", lambda to: s3u.at[to], rhu, zh, "zh_")
    go(dkv_copies[3])
    s4d[...] = sum_of_four(s3d[zh], rhd, zhd)
    zld = to_three("zld", lambda to: s4d.at[div(to, 2)], rld, zl, "zl_")
    s4u[...] = sum_of_four(s3u[zh], rhu, zhu)
    zlu = to_three("zlu", lambda to: s4u, rlu, zl, "zl_")

    early = list(sent)
    last = []
    fd[y] = sum_of_four(s4d[div(zl, 2)], rld, zld)
    for k in (2, 1, 3):
        last.append(remote(fd.at[y], fd.at[y], SEM["xyd"] + k - 1, dev(y_=mod(y + k, 4))))
        last[-1].start()
    fu[y, x] = sum_of_four(s4u[...], rlu, zlu)
    for n, (i, j) in enumerate(plane):
        to = dev(y_=mod(y + i, 4), x_=mod(x + j, 4))
        last.append(remote(fu.at[y, x], fu.at[y, x], SEM["xyu"] + n, to))
        last[-1].start()

    for copy in early:
        copy.wait_send()
    for i in range(KV):
        dkv_copies[i].wait_recv()
        at = slice(i * HEAD, (i + 1) * HEAD)
        kg_v[0, :, at] = (dkv_own[i, 0] + dkv_in[i, 0].astype(F32)).astype(BF16)
        vg_v[0, :, at] = (dkv_own[i, 1] + dkv_in[i, 1].astype(F32)).astype(BF16)
    results = [local(kg_v, kg_o, L_OUT), local(vg_v, vg_o, L_OUT + 1)]
    for copy in results:
        copy.start()

    for copy in last + tens:
        copy.wait_recv()
    odd = jnp.broadcast_to(mod(zl, 2), (R, 64)) > 0
    for a in range(TEN):
        down = jnp.zeros((R, 128), F32)
        for j in range(4):
            down += jnp.where(ten_v[j].astype(F32) == a, fd[j].astype(F32), 0.0)
        down_v[a] = jnp.where(odd, down[:, 64:], down[:, :64])
        for k in range(4):
            up = jnp.zeros((R, 128), F32)
            for j in range(4):
                up += jnp.where(ten_v[j].astype(F32) == a, fu[j, k].astype(F32), 0.0)
            up_v[a, :, k * 128:(k + 1) * 128] = up

    results += [local(down_v, down_o, L_OUT + 2), local(up_v, up_o, L_OUT + 3)]
    for copy in results[2:]:
        copy.start()
    for copy in last:
        copy.wait_send()
    for copy in results:
        copy.wait()


def hand_over(*refs):
    given, taken, held, sems = refs[:4], refs[4:8], refs[8:12], refs[12]
    inward = [pltpu.make_async_copy(given[i], held[i], sems.at[0, i]) for i in range(4)]
    outward = [pltpu.make_async_copy(held[i], taken[i], sems.at[1, i]) for i in range(4)]
    for copy in inward:
        copy.start()
    for before, after in zip(inward, outward):
        before.wait()
        after.start()
    for copy in outward:
        copy.wait()


def local(queries, keys, values, output_gradient, layer_input, saved_log_total, row_dot_products, segment_ids, tenants,
          adapter_down, adapter_up):
    anywhere = pl.BlockSpec(memory_space=pl.ANY)
    results = (
        jax.ShapeDtypeStruct((1, TOK, KV * HEAD), BF16),
        jax.ShapeDtypeStruct((1, TOK, KV * HEAD), BF16),
        jax.ShapeDtypeStruct((TEN, R, 64), F32),
        jax.ShapeDtypeStruct((TEN, R, 512), F32),
    )
    raw = pl.pallas_call(
        kernel,
        out_shape=results,
        in_specs=[pl.BlockSpec(memory_space=pltpu.SMEM)] + [anywhere] * 10,
        out_specs=(anywhere,) * 4,
        scratch_shapes=[
            pltpu.VMEM((TOK, WIDE), BF16),
            pltpu.VMEM((TOK, WIDE), BF16),
            pltpu.VMEM((TOK, D), BF16),
            pltpu.VMEM((KV, 2, TOK, HEAD), BF16),
            pltpu.VMEM((KV, 2, TOK, HEAD), BF16),
            pltpu.VMEM((2, 4, 1024), F32),
            pltpu.VMEM((8, 2, 4, TOK), F32),
            pltpu.VMEM((2, 1, TOK), jnp.int32),
            pltpu.VMEM((TEN, R, 64), BF16),
            pltpu.VMEM((TEN, R, 512), BF16),
            pltpu.VMEM((2 * TOK, TOK), F32),
            pltpu.VMEM((KV, 2, TOK, HEAD), F32),
            pltpu.VMEM((KV, 2, TOK, HEAD), BF16),
            pltpu.VMEM((KV, 2, TOK, HEAD), BF16),
            pltpu.VMEM((WIDE, TOK), BF16),
            pltpu.VMEM((8, 2, R, 128), BF16),
            pltpu.VMEM((4, 4, 4, R, 128), BF16),
            pltpu.VMEM((4, 8, R, 128), BF16),
            pltpu.VMEM((4, R, 128), BF16),
            pltpu.VMEM((2, 4, 4, R, 128), BF16),
            pltpu.VMEM((2, 4, 4, 2, R, 128), BF16),
            pltpu.VMEM((4, 4, R, 128), BF16),
            pltpu.VMEM((4, 4, 2, R, 128), BF16),
            pltpu.VMEM((4, 4, R, 128), BF16),
            pltpu.VMEM((4, 4, 2, R, 128), BF16),
            pltpu.VMEM((3, 4, R, 128), BF16),
            pltpu.VMEM((3, 4, 2, R, 128), BF16),
            pltpu.VMEM((4, R, 128), BF16),
            pltpu.VMEM((4, 2, R, 128), BF16),
            pltpu.VMEM((3, R, 128), BF16),
            pltpu.VMEM((3, 2, R, 128), BF16),
            pltpu.VMEM((R, 128), BF16),
            pltpu.VMEM((2, R, 128), BF16),
            pltpu.VMEM((3, R, 128), BF16),
            pltpu.VMEM((3, R, 128), BF16),
            pltpu.VMEM((4, 4, R, 128), BF16),
            pltpu.VMEM((4, R, 128), BF16),
            pltpu.VMEM((1, TOK, KV * HEAD), BF16),
            pltpu.VMEM((1, TOK, KV * HEAD), BF16),
            pltpu.VMEM((TEN, R, 64), F32),
            pltpu.VMEM((TEN, R, 512), F32),
            pltpu.SemaphoreType.DMA((N_LOC,)),
            pltpu.SemaphoreType.DMA((N_SEM,)),
            pltpu.SemaphoreType.DMA((N_SEM,)),
        ],
        compiler_params=pltpu.CompilerParams(
            collective_id=0, has_side_effects=True, vmem_limit_bytes=60 * 1024 * 1024
        ),
        cost_estimate=pl.CostEstimate(flops=1_500_000_000, bytes_accessed=5_000_000, transcendentals=1_048_576),
    )(
        tenants, queries, keys, values, output_gradient, layer_input, saved_log_total, row_dot_products, segment_ids,
        jnp.swapaxes(adapter_down, 1, 2), adapter_up,
    )
    key_grad, value_grad, down_grad, up_grad = pl.pallas_call(
        hand_over,
        out_shape=results,
        in_specs=[anywhere] * 4,
        out_specs=(anywhere,) * 4,
        scratch_shapes=[pltpu.VMEM(r.shape, r.dtype) for r in results] + [pltpu.SemaphoreType.DMA((2, 4))],
        compiler_params=pltpu.CompilerParams(vmem_limit_bytes=60 * 1024 * 1024),
        cost_estimate=pl.CostEstimate(flops=0, bytes_accessed=1_000_000, transcendentals=0),
    )(*raw)
    return key_grad, value_grad, jnp.swapaxes(down_grad, 1, 2), up_grad


def solution(mesh):
    tokens = P("dp", ("blk", "uly"), None)
    rows = P("dp", "uly", "blk")
    return jax.shard_map(
        local,
        mesh=mesh,
        in_specs=(
            tokens, tokens, tokens, tokens, tokens, rows, rows, P("dp", None), P("dp"),
            P(None, ("blk", "uly"), None), P(None, None, "uly"),
        ),
        out_specs=(tokens, tokens, P(None, ("blk", "uly"), None), P(None, None, "uly")),
        check_vma=False,
    )
```
